32 devices in a mesh: blk: 8 (over z, y), team: 4 (over x, core).
Axes of the slice: x: 2, y: 2, z: 4, core: 2. Of those that a mesh axis runs over, the one named last changes fastest.
Arguments:
- omega: float32 [8, 8, 128, 128], P('blk'), may hold values from -0.05 to 2, as said below
- dosage: float32 [8, 256, 128], P('blk', 'team'), may hold values from -6 to 6
- columns: int32 [8, 8], P('blk'), may hold values from 0 to 7, as said below
- counts: int32 [8], P('blk'), may hold values from 1 to 4, as said below
Outputs:
- new_omega: float32 [8, 8, 128, 128], P('blk')
- y_product: float32 [8, 256, 128], P('blk', 'team')
The draws below stay inside these ranges and needn't reach their ends.
Inputs may be any that keep to these rules, and one draw needn't show every extreme that they name: The first counts[b] slots of row b hold distinct block columns in ascending order, b among them; the pattern is symmetric (c is listed in row b exactly when b is listed in row c); every live column c of row b has |c - b| <= 1, or (c - b) mod 8 equal to f or 8 - f for one of the offsets f = 4 - j * 2, j = 0 to 0, and every row is linked at all these distant offsets; the other slots hold b. `counts`: some block row has exactly 4 in every draw. `omega`: symmetric: the block in row b for column c is the transpose of the block in row c for column b; diagonal entries of diagonal blocks lie in 1 to 2, all other entries in -0.05 to 0.05.
All inputs are finite; a program needn't handle non-finite values.
Results may differ from the reference program's by a relative error of at most 0.0003.
Values sent between devices are 32-bit elements; how exact they have to be, the bound alone decides.
A program may use at most 64 MiB of HBM per device.

```python
import jax
import jax.numpy as jnp
from jax import lax

BLOCK = 128
ROWBLOCKS = 8
SAMPLES = 256
BAND = 1
FARLINKS = 1
FARSTEP = 2
SLOTS = 8


def link_pattern(key):
    base = jax.random.fold_in(key, 7)
    key_width, key_run = jax.random.split(base, 2)
    rolled = jax.random.randint(key_width, (ROWBLOCKS,), 0, BAND + 1)
    widths = rolled * rolled // BAND
    first = jax.random.randint(key_run, (), 0, ROWBLOCKS - 2 * BAND)
    rows = jnp.arange(ROWBLOCKS)
    inside = (rows >= first) & (rows <= first + 2 * BAND)
    widths = jnp.where(inside, BAND, widths)
    far = ROWBLOCKS // 2 - jnp.arange(FARLINKS) * FARSTEP
    offset = rows[None, :] - rows[:, None]
    near = jnp.abs(offset) <= jnp.minimum(widths[:, None], widths[None, :])
    wrapped = jnp.mod(offset, ROWBLOCKS)
    distant = jnp.any((wrapped[:, :, None] == far[None, None, :]) | (wrapped[:, :, None] == ROWBLOCKS - far[None, None, :]), axis=2)
    linked = near | distant
    link_counts = jnp.sum(linked, axis=1).astype(jnp.int32)
    ordered = jnp.sort(jnp.where(linked, rows[None, :], ROWBLOCKS + rows[None, :]), axis=1)[:, :SLOTS]
    link_columns = jnp.where(ordered >= ROWBLOCKS, rows[:, None], ordered).astype(jnp.int32)
    return (link_columns, link_counts)


def draw_columns(key, part):
    return link_pattern(key)[0]


def draw_counts(key, part):
    return link_pattern(key)[1]


def draw_omega(key, part):
    link_columns, link_counts = link_pattern(key)
    rows = jnp.broadcast_to(jnp.arange(ROWBLOCKS)[:, None], link_columns.shape)
    lower = jnp.minimum(rows, link_columns)
    upper = jnp.maximum(rows, link_columns)
    flipped = rows > link_columns
    base = jax.random.fold_in(key, 11)

    def one_block(low, high, flip):
        block_key = jax.random.fold_in(base, low * ROWBLOCKS + high)
        values = jnp.clip(jax.random.normal(block_key, (BLOCK, BLOCK), jnp.float32), -5.0, 5.0) * 0.01
        values = jnp.where(flip, values.T, values)
        mirrored = (values + values.T) * 0.5
        diag_values = jax.random.uniform(jax.random.fold_in(block_key, 1), (BLOCK,), jnp.float32, 1.0, 2.0)
        unit = jnp.eye(BLOCK, dtype=bool)
        diagonal_block = jnp.where(unit, diag_values[:, None], mirrored)
        return jnp.where(low == high, diagonal_block, values)
    return jax.vmap(jax.vmap(one_block))(lower, upper, flipped)


def steps_of(own_key, extent, pieces, low, high):
    def one(dim, blocks):
        heights = jax.random.uniform(jax.random.fold_in(jax.random.fold_in(own_key, 6), dim), (blocks,), jnp.float32, low / len(pieces), high / len(pieces))
        return jnp.repeat(jnp.exp(heights), extent[dim] // blocks).reshape((-1,) + (1,) * (len(extent) - dim - 1))

    loudness = one(*pieces[0])
    for cut in pieces[1:]:
        loudness = loudness * one(*cut)
    return loudness


def centred(stream_key, extent, spread, reach, shards=(), kind=jnp.bfloat16):
    entries = spread * jax.random.normal(stream_key, extent, jnp.float32)
    if shards:
        entries = entries * steps_of(stream_key, extent, shards, -0.22, 0.18)
    return jnp.clip(entries, -reach, reach).astype(kind)


def setup_inputs(seed: int = 0) -> dict:
    arg_keys = jax.random.split(jax.random.key(seed), 5)
    return {
        "omega": draw_omega(jax.random.fold_in(arg_keys[4], 71), 0),
        "dosage": centred(arg_keys[1], (ROWBLOCKS, SAMPLES, BLOCK), 1.0, 6.0, ((0, 8), (1, 4)), jnp.float32),
        "columns": draw_columns(jax.random.fold_in(arg_keys[4], 71), 0),
        "counts": draw_counts(jax.random.fold_in(arg_keys[4], 71), 0),
    }


step_size = 0.1
penalty = 0.05


def reference(omega, dosage, columns, counts):
    highest = lax.Precision.HIGHEST
    slot_ids = jnp.arange(SLOTS).astype(jnp.int32)
    live = slot_ids[None, :] < counts[:, None]
    row_ids = jnp.arange(ROWBLOCKS).astype(jnp.int32)

    def product_row(row):
        picked = jnp.where(live[row][:, None, None], dosage[columns[row]], 0.0)
        return jnp.einsum('ksb,kab->sa', picked, omega[row], precision=highest)

    y_product = lax.map(product_row, row_ids)
    unit = jnp.eye(BLOCK, dtype=bool)

    def update_row(row):
        keep = live[row]
        links = columns[row]
        far_dosage = jnp.where(keep[:, None, None], dosage[links], 0.0)
        far_product = jnp.where(keep[:, None, None], y_product[links], 0.0)
        grad = jnp.einsum('sa,ksb->kab', y_product[row], far_dosage, precision=highest)
        grad = grad + jnp.einsum('sa,ksb->kab', dosage[row], far_product, precision=highest)
        grad = grad / (2.0 * SAMPLES)
        on_diag = keep & (links == row)
        diag_values = jnp.sum(jnp.where(on_diag[:, None], jnp.diagonal(omega[row], axis1=1, axis2=2), 0.0), axis=0)
        corner = on_diag[:, None, None] & unit[None]
        grad = grad - jnp.where(corner, 1.0 / diag_values[None, None, :], 0.0)
        moved = omega[row] - step_size * grad
        shrunk = jnp.sign(moved) * jnp.maximum(jnp.abs(moved) - step_size * penalty, 0.0)
        result = jnp.where(corner, moved, shrunk)
        return jnp.where(keep[:, None, None], result, 0.0)

    new_omega = lax.map(update_row, row_ids)
    return new_omega, y_product
```

```python
import jax
import jax.numpy as jnp
from jax import lax
from jax.experimental import pallas as pl
from jax.experimental.pallas import tpu as pltpu
from jax.sharding import PartitionSpec as P

step_size = 0.1
penalty = 0.05
MESH = pl.DeviceIdType.MESH


def link_distances(row_total):
    reach_near = max(1, row_total // 16)
    far_count = max(1, row_total // 32)
    far_stride = max(1, (row_total // 2 - 1 - reach_near) // far_count)
    distances = [(0, False)]
    for distance in range(1, reach_near + 1):
        distances.append((distance, False))
        distances.append((-distance, False))
    for number in range(far_count):
        distance = row_total // 2 - number * far_stride
        distances.append((distance, True))
        if 2 * distance != row_total:
            distances.append((-distance, True))
    return distances


def split(value):
    high = value.astype(jnp.bfloat16)
    low = (value - high.astype(jnp.float32)).astype(jnp.bfloat16)
    return high, low


def make_kernel(row_total, team_size, slot_count, samples_here, size):
    distances = link_distances(row_total)
    tiles = len(distances)
    used = min(slot_count, tiles)
    groups = team_size // 2
    half_rows = size // 2
    samples = samples_here * team_size

    def kernel(links, counts, w_hbm, x_hbm, out_hbm, y_hbm,
               w_buf, x_buf, y_buf, part, pair_in, half, far_in, full, out_buf,
               local_sem, x_send, x_recv, y_send, y_recv, pair_send, pair_recv,
               far_send, far_recv, full_send, full_recv):
        row = lax.axis_index("blk")
        team = lax.axis_index("team")
        core = lax.rem(team, 2)
        group = team // 2
        other = group * 2 + (1 - core)
        mine = pl.ds(pl.multiple_of(core * half_rows, half_rows), half_rows)
        theirs = pl.ds(pl.multiple_of((1 - core) * half_rows, half_rows), half_rows)

        load_w = pltpu.make_async_copy(w_hbm.at[0, pl.ds(0, used)], w_buf, local_sem.at[0])
        load_w.start()
        load_x = pltpu.make_async_copy(x_hbm.at[0], x_buf.at[0], local_sem.at[1])
        load_x.start()

        def target(t):
            distance, wraps = distances[t]
            there = row - distance
            ok = None if wraps else (there >= 0) & (there < row_total)
            return lax.rem(there + row_total, row_total), ok

        def source_ok(t):
            distance, wraps = distances[t]
            there = row + distance
            return None if wraps else (there >= 0) & (there < row_total)

        def guarded(ok, action):
            if ok is None:
                action()
            else:
                pl.when(ok)(action)

        def far_team(step):
            return lax.rem(group + step, groups) * 2 + core

        barrier = pltpu.get_barrier_semaphore()
        expected = jnp.int32(groups)
        for t in range(1, tiles):
            there, ok = target(t)

            def greet(there=there):
                pl.semaphore_signal(barrier, inc=1, device_id=(there, team), device_id_type=MESH)
            guarded(ok, greet)
            back = source_ok(t)
            expected = expected + (1 if back is None else back.astype(jnp.int32))
        pl.semaphore_signal(barrier, inc=1, device_id=(row, other), device_id_type=MESH)
        for step in range(1, groups):
            pl.semaphore_signal(barrier, inc=1, device_id=(row, far_team(step)), device_id_type=MESH)
        pl.semaphore_wait(barrier, expected)

        def exchange(source, buf, send, recv):
            copies = [None]
            for t in range(1, tiles):
                there, ok = target(t)
                copy = pltpu.make_async_remote_copy(
                    src_ref=source, dst_ref=buf.at[t], send_sem=send.at[t], recv_sem=recv.at[t],
                    device_id=(there, team), device_id_type=MESH)
                guarded(ok, copy.start)
                copies.append(copy)
            return copies

        def arrived(copies, buf, t):
            ok = source_ok(t)
            if ok is None:
                copies[t].wait_recv()
            else:
                pl.when(ok)(copies[t].wait_recv)

                def clear():
                    buf[t] = jnp.zeros_like(buf[t])
                pl.when(jnp.logical_not(ok))(clear)

        def sent(copies):
            for t in range(1, tiles):
                guarded(target(t)[1], copies[t].wait_send)

        x_copies = exchange(x_hbm.at[0], x_buf, x_send, x_recv)

        rest = slot_count - used
        clear_rest = None
        if rest:
            out_buf[pl.ds(used, rest)] = jnp.zeros((rest, size, size), jnp.float32)
            clear_rest = pltpu.make_async_copy(
                out_buf.at[pl.ds(used, rest)], out_hbm.at[0, pl.ds(used, rest)], local_sem.at[3])
            clear_rest.start()

        live_count = counts[0]
        slot_of, is_live = [], []
        for t in range(tiles):
            column = lax.rem(row + distances[t][0] + row_total, row_total)
            slot = jnp.int32(0)
            found = jnp.bool_(False)
            for k in range(used):
                hit = (links[0, k] == column) & (k < live_count)
                slot = jnp.where(hit, k, slot)
                found = found | hit
            slot_of.append(slot)
            is_live.append(found)

        load_w.wait()
        load_x.wait()
        y = None
        for t in range(tiles):
            weight = jnp.where(is_live[t], w_buf[slot_of[t]], 0.0)
            w_high, w_low = split(weight)
            right = jnp.concatenate([w_high, w_low, w_high], axis=1)
            if t:
                arrived(x_copies, x_buf, t)
            high, low = split(x_buf[t])
            left = jnp.concatenate([high, high, low], axis=1)
            term = lax.dot_general(left, right, (((1,), (1,)), ((), ())),
                                   preferred_element_type=jnp.float32)
            y = term if y is None else y + term
        y_buf[0] = y
        y_copies = exchange(y_buf.at[0], y_buf, y_send, y_recv)
        store_y = pltpu.make_async_copy(y_buf.at[0], y_hbm.at[0], local_sem.at[2])
        store_y.start()

        both = jnp.concatenate([y, x_buf[0]], axis=0).T
        high, low = split(both)
        left = jnp.concatenate([high, high, low], axis=1)

        pair_copies, far_copies, full_copies = [], [], []

        def stage_tile(t):
            if t:
                arrived(y_copies, y_buf, t)
            high, low = split(jnp.concatenate([x_buf[t], y_buf[t]], axis=0))
            right = jnp.concatenate([high, low, high], axis=0)
            part[t] = jnp.dot(left, right, preferred_element_type=jnp.float32)
            copy = pltpu.make_async_remote_copy(
                src_ref=part.at[t, theirs], dst_ref=pair_in.at[t],
                send_sem=pair_send.at[t], recv_sem=pair_recv.at[t],
                device_id=(row, other), device_id_type=MESH)
            copy.start()
            pair_copies.append(copy)

        def stage_pair(t):
            pair_copies[t].wait_recv()
            half[t] = part[t, mine] + pair_in[t]
            row_copies = []
            for step in range(1, groups):
                copy = pltpu.make_async_remote_copy(
                    src_ref=half.at[t], dst_ref=far_in.at[step - 1, t],
                    send_sem=far_send.at[step - 1, t], recv_sem=far_recv.at[step - 1, t],
                    device_id=(row, far_team(step)), device_id_type=MESH)
                copy.start()
                row_copies.append(copy)
            far_copies.append(row_copies)

        def stage_far(t):
            total = half[t]
            for step in range(1, groups):
                far_copies[t][step - 1].wait_recv()
                total = total + far_in[step - 1, t]
            full[t, mine] = total
            copy = pltpu.make_async_remote_copy(
                src_ref=full.at[t, mine], dst_ref=full.at[t, mine],
                send_sem=full_send.at[t], recv_sem=full_recv.at[t],
                device_id=(row, other), device_id_type=MESH)
            copy.start()
            full_copies.append(copy)

        stage_tile(0)
        stage_pair(0)
        for t in range(1, tiles):
            stage_tile(t)
        for t in range(1, tiles):
            stage_pair(t)
        for t in range(tiles):
            stage_far(t)
        for t in range(tiles):
            full_copies[t].wait_recv()

        diagonal = (lax.broadcasted_iota(jnp.int32, (size, size), 0)
                    == lax.broadcasted_iota(jnp.int32, (size, size), 1))
        stores = []
        for k in range(used):
            live = k < live_count
            column = links[0, k]
            place = jnp.int32(0)
            for t in range(1, tiles):
                hit = column == lax.rem(row + distances[t][0] + row_total, row_total)
                place = jnp.where(hit, t, place)
            weight = w_buf[k]
            grad = full[place] / (2.0 * samples)
            corner = diagonal & (live & (column == row))
            grad = grad - jnp.where(corner, 1.0 / jnp.where(corner, weight, 1.0), 0.0)
            moved = weight - step_size * grad
            edge = step_size * penalty
            shrunk = moved - jnp.minimum(jnp.maximum(moved, -edge), edge)
            result = jnp.where(corner, moved, shrunk)
            out_buf[k] = jnp.where(live, result, 0.0)
            copy = pltpu.make_async_copy(out_buf.at[k], out_hbm.at[0, k], local_sem.at[4 + k])
            copy.start()
            stores.append(copy)

        sent(x_copies)
        sent(y_copies)
        for t in range(tiles):
            pair_copies[t].wait_send()
            for copy in far_copies[t]:
                copy.wait_send()
            full_copies[t].wait_send()
        store_y.wait()
        if clear_rest is not None:
            clear_rest.wait()
        for copy in stores:
            copy.wait()

    f32 = jnp.float32
    far = max(1, groups - 1)
    dma = pltpu.SemaphoreType.DMA
    scratch = [
        pltpu.VMEM((used, size, size), f32),
        pltpu.VMEM((tiles, samples_here, size), f32),
        pltpu.VMEM((tiles, samples_here, size), f32),
        pltpu.VMEM((tiles, size, size), f32),
        pltpu.VMEM((tiles, half_rows, size), f32),
        pltpu.VMEM((tiles, half_rows, size), f32),
        pltpu.VMEM((far, tiles, half_rows, size), f32),
        pltpu.VMEM((tiles, size, size), f32),
        pltpu.VMEM((slot_count, size, size), f32),
        dma((4 + used,)), dma((tiles,)), dma((tiles,)), dma((tiles,)), dma((tiles,)),
        dma((tiles,)), dma((tiles,)), dma((far, tiles)), dma((far, tiles)),
        dma((tiles,)), dma((tiles,)),
    ]
    return kernel, scratch


def per_device(omega, dosage, columns, counts):
    row_total = lax.axis_size("blk")
    team_size = lax.axis_size("team")
    slot_count, size = omega.shape[1], omega.shape[2]
    samples_here = dosage.shape[1]
    kernel, scratch = make_kernel(row_total, team_size, slot_count, samples_here, size)
    return pl.pallas_call(
        kernel,
        out_shape=(jax.ShapeDtypeStruct(omega.shape, jnp.float32),
                   jax.ShapeDtypeStruct(dosage.shape, jnp.float32)),
        in_specs=[pl.BlockSpec(memory_space=pltpu.SMEM), pl.BlockSpec(memory_space=pltpu.SMEM),
                  pl.BlockSpec(memory_space=pl.ANY), pl.BlockSpec(memory_space=pl.ANY)],
        out_specs=(pl.BlockSpec(memory_space=pl.ANY), pl.BlockSpec(memory_space=pl.ANY)),
        scratch_shapes=scratch,
        compiler_params=pltpu.CompilerParams(
            collective_id=0, has_side_effects=True, vmem_limit_bytes=32 * 1024 * 1024),
    )(columns, counts, omega, dosage)


def solution(mesh):
    return jax.shard_map(
        per_device,
        mesh=mesh,
        in_specs=(P("blk", None, None, None), P("blk", "team", None), P("blk", None), P("blk")),
        out_specs=(P("blk", None, None, None), P("blk", "team", None)),
        check_vma=False,
    )
```

```python
import jax
import jax.numpy as jnp
from jax import lax
from jax.experimental import pallas as pl
from jax.experimental.pallas import tpu as pltpu
from jax.sharding import PartitionSpec as P

step_size = 0.1
penalty = 0.05
MESH = pl.DeviceIdType.MESH


def link_distances(row_total):
    reach_near = max(1, row_total // 16)
    far_count = max(1, row_total // 32)
    far_stride = max(1, (row_total // 2 - 1 - reach_near) // far_count)
    distances = [(0, False)]
    for distance in range(1, reach_near + 1):
        distances.append((distance, False))
        distances.append((-distance, False))
    for number in range(far_count):
        distance = row_total // 2 - number * far_stride
        distances.append((distance, True))
        if 2 * distance != row_total:
            distances.append((-distance, True))
    return distances


def split(value):
    high = value.astype(jnp.bfloat16)
    low = (value - high.astype(jnp.float32)).astype(jnp.bfloat16)
    return high, low


def make_kernel(row_total, team_size, slot_count, samples_here, size):
    distances = link_distances(row_total)
    tiles = len(distances)
    used = min(slot_count, tiles)
    groups = team_size // 2
    half_rows = size // 2
    samples = samples_here * team_size

    def kernel(links_hbm, w_hbm, x_hbm, out_buf, y_out,
               links, w_buf, x_buf, y_buf, part, pair_in, half, far_in, full,
               local_sem, x_send, x_recv, y_send, y_recv, pair_send, pair_recv,
               far_send, far_recv, full_send, full_recv):
        row = lax.axis_index("blk")
        team = lax.axis_index("team")
        core = lax.rem(team, 2)
        group = team // 2
        other = group * 2 + (1 - core)
        mine = pl.ds(pl.multiple_of(core * half_rows, half_rows), half_rows)
        theirs = pl.ds(pl.multiple_of((1 - core) * half_rows, half_rows), half_rows)

        load_w = pltpu.make_async_copy(w_hbm.at[0, pl.ds(0, used)], w_buf, local_sem.at[0])
        load_w.start()
        load_x = pltpu.make_async_copy(x_hbm.at[0], x_buf.at[0], local_sem.at[1])
        load_x.start()
        load_links = pltpu.make_async_copy(links_hbm, links, local_sem.at[2])
        load_links.start()

        def target(t):
            distance, wraps = distances[t]
            there = row - distance
            ok = None if wraps else (there >= 0) & (there < row_total)
            return lax.rem(there + row_total, row_total), ok

        def source_ok(t):
            distance, wraps = distances[t]
            there = row + distance
            return None if wraps else (there >= 0) & (there < row_total)

        def guarded(ok, action):
            if ok is None:
                action()
            else:
                pl.when(ok)(action)

        def far_team(step):
            return lax.rem(group + step, groups) * 2 + core

        barrier = pltpu.get_barrier_semaphore()
        expected = jnp.int32(groups)
        for t in range(1, tiles):
            there, ok = target(t)

            def greet(there=there):
                pl.semaphore_signal(barrier, inc=1, device_id=(there, team), device_id_type=MESH)
            guarded(ok, greet)
            back = source_ok(t)
            expected = expected + (1 if back is None else back.astype(jnp.int32))
        pl.semaphore_signal(barrier, inc=1, device_id=(row, other), device_id_type=MESH)
        for step in range(1, groups):
            pl.semaphore_signal(barrier, inc=1, device_id=(row, far_team(step)), device_id_type=MESH)
        pl.semaphore_wait(barrier, expected)

        def exchange(source, buf, send, recv):
            copies = [None]
            for t in range(1, tiles):
                there, ok = target(t)
                copy = pltpu.make_async_remote_copy(
                    src_ref=source, dst_ref=buf.at[t], send_sem=send.at[t], recv_sem=recv.at[t],
                    device_id=(there, team), device_id_type=MESH)
                guarded(ok, copy.start)
                copies.append(copy)
            return copies

        def arrived(copies, buf, t):
            ok = source_ok(t)
            if ok is None:
                copies[t].wait_recv()
            else:
                pl.when(ok)(copies[t].wait_recv)

                def clear():
                    buf[t] = jnp.zeros_like(buf[t])
                pl.when(jnp.logical_not(ok))(clear)

        def sent(copies):
            for t in range(1, tiles):
                guarded(target(t)[1], copies[t].wait_send)

        x_copies = exchange(x_hbm.at[0], x_buf, x_send, x_recv)

        rest = slot_count - used
        if rest:
            out_buf[0, pl.ds(used, rest)] = jnp.zeros((rest, size, size), jnp.float32)

        load_links.wait()
        live_slot = [jnp.bool_(True)] + [links[0, k] > links[0, k - 1] for k in range(1, used)]
        slot_of, is_live = [], []
        for t in range(tiles):
            column = lax.rem(row + distances[t][0] + row_total, row_total)
            slot = jnp.int32(0)
            found = jnp.bool_(False)
            for k in range(used):
                hit = (links[0, k] == column) & live_slot[k]
                slot = jnp.where(hit, k, slot)
                found = found | hit
            slot_of.append(slot)
            is_live.append(found)

        load_w.wait()
        load_x.wait()
        y = None
        for t in range(tiles):
            weight = jnp.where(is_live[t], w_buf[slot_of[t]], 0.0)
            w_high, w_low = split(weight)
            right = jnp.concatenate([w_high, w_low, w_high], axis=1)
            if t:
                arrived(x_copies, x_buf, t)
            high, low = split(x_buf[t])
            left = jnp.concatenate([high, high, low], axis=1)
            term = lax.dot_general(left, right, (((1,), (1,)), ((), ())),
                                   preferred_element_type=jnp.float32)
            y = term if y is None else y + term
        y_buf[0] = y
        y_copies = exchange(y_buf.at[0], y_buf, y_send, y_recv)
        y_out[0] = y

        both = jnp.concatenate([y, x_buf[0]], axis=0).T
        high, low = split(both)
        left = jnp.concatenate([high, high, low], axis=1)

        pair_copies, far_copies, full_copies = [], [], []

        def stage_tile(t):
            if t:
                arrived(y_copies, y_buf, t)
            high, low = split(jnp.concatenate([x_buf[t], y_buf[t]], axis=0))
            right = jnp.concatenate([high, low, high], axis=0)
            part[t] = jnp.dot(left, right, preferred_element_type=jnp.float32)
            copy = pltpu.make_async_remote_copy(
                src_ref=part.at[t, theirs], dst_ref=pair_in.at[t],
                send_sem=pair_send.at[t], recv_sem=pair_recv.at[t],
                device_id=(row, other), device_id_type=MESH)
            copy.start()
            pair_copies.append(copy)

        def stage_pair(t):
            pair_copies[t].wait_recv()
            half[t] = part[t, mine] + pair_in[t]
            row_copies = []
            for step in range(1, groups):
                copy = pltpu.make_async_remote_copy(
                    src_ref=half.at[t], dst_ref=far_in.at[step - 1, t],
                    send_sem=far_send.at[step - 1, t], recv_sem=far_recv.at[step - 1, t],
                    device_id=(row, far_team(step)), device_id_type=MESH)
                copy.start()
                row_copies.append(copy)
            far_copies.append(row_copies)

        def stage_far(t):
            total = half[t]
            for step in range(1, groups):
                far_copies[t][step - 1].wait_recv()
                total = total + far_in[step - 1, t]
            full[t, mine] = total
            copy = pltpu.make_async_remote_copy(
                src_ref=full.at[t, mine], dst_ref=full.at[t, mine],
                send_sem=full_send.at[t], recv_sem=full_recv.at[t],
                device_id=(row, other), device_id_type=MESH)
            copy.start()
            full_copies.append(copy)

        stage_tile(0)
        stage_pair(0)
        for t in range(1, tiles):
            stage_tile(t)
        for t in range(1, tiles):
            stage_pair(t)
        for t in range(tiles):
            stage_far(t)
        for t in range(tiles):
            full_copies[t].wait_recv()

        diagonal = (lax.broadcasted_iota(jnp.int32, (size, size), 0)
                    == lax.broadcasted_iota(jnp.int32, (size, size), 1))
        for k in range(used):
            live = live_slot[k]
            column = links[0, k]
            place = jnp.int32(0)
            for t in range(1, tiles):
                hit = column == lax.rem(row + distances[t][0] + row_total, row_total)
                place = jnp.where(hit, t, place)
            weight = w_buf[k]
            grad = full[place] / (2.0 * samples)
            corner = diagonal & (live & (column == row))
            grad = grad - jnp.where(corner, 1.0 / jnp.where(corner, weight, 1.0), 0.0)
            moved = weight - step_size * grad
            edge = step_size * penalty
            shrunk = moved - jnp.minimum(jnp.maximum(moved, -edge), edge)
            result = jnp.where(corner, moved, shrunk)
            out_buf[0, k] = jnp.where(live, result, 0.0)

        sent(x_copies)
        sent(y_copies)
        for t in range(tiles):
            pair_copies[t].wait_send()
            for copy in far_copies[t]:
                copy.wait_send()
            full_copies[t].wait_send()

    f32 = jnp.float32
    far = max(1, groups - 1)
    dma = pltpu.SemaphoreType.DMA
    scratch = [
        pltpu.SMEM((1, slot_count), jnp.int32),
        pltpu.VMEM((used, size, size), f32),
        pltpu.VMEM((tiles, samples_here, size), f32),
        pltpu.VMEM((tiles, samples_here, size), f32),
        pltpu.VMEM((tiles, size, size), f32),
        pltpu.VMEM((tiles, half_rows, size), f32),
        pltpu.VMEM((tiles, half_rows, size), f32),
        pltpu.VMEM((far, tiles, half_rows, size), f32),
        pltpu.VMEM((tiles, size, size), f32),
        dma((3,)), dma((tiles,)), dma((tiles,)), dma((tiles,)), dma((tiles,)),
        dma((tiles,)), dma((tiles,)), dma((far, tiles)), dma((far, tiles)),
        dma((tiles,)), dma((tiles,)),
    ]
    return kernel, scratch


def write_out(omega_in, y_in, omega_out, y_out, sem):
    first = pltpu.make_async_copy(omega_in, omega_out, sem.at[0])
    second = pltpu.make_async_copy(y_in, y_out, sem.at[1])
    first.start()
    second.start()
    first.wait()
    second.wait()


def per_device(omega, dosage, columns, counts):
    row_total = lax.axis_size("blk")
    team_size = lax.axis_size("team")
    slot_count, size = omega.shape[1], omega.shape[2]
    samples_here = dosage.shape[1]
    kernel, scratch = make_kernel(row_total, team_size, slot_count, samples_here, size)
    shapes = (jax.ShapeDtypeStruct(omega.shape, jnp.float32),
              jax.ShapeDtypeStruct(dosage.shape, jnp.float32))
    results = pl.pallas_call(
        kernel,
        out_shape=shapes,
        in_specs=[pl.BlockSpec(memory_space=pltpu.HBM)] * 3,
        out_specs=(pl.BlockSpec(memory_space=pltpu.VMEM), pl.BlockSpec(memory_space=pltpu.VMEM)),
        scratch_shapes=scratch,
        compiler_params=pltpu.CompilerParams(
            collective_id=0, has_side_effects=True, vmem_limit_bytes=24 * 1024 * 1024),
    )(*[pltpu.with_memory_space_constraint(value, pltpu.HBM)
        for value in (columns, omega, dosage)])
    return pl.pallas_call(
        write_out,
        out_shape=shapes,
        in_specs=[pl.BlockSpec(memory_space=pl.ANY)] * 2,
        out_specs=(pl.BlockSpec(memory_space=pltpu.HBM), pl.BlockSpec(memory_space=pltpu.HBM)),
        scratch_shapes=[pltpu.SemaphoreType.DMA((2,))],
    )(*[pltpu.with_memory_space_constraint(value, pltpu.VMEM) for value in results])


def solution(mesh):
    return jax.shard_map(
        per_device,
        mesh=mesh,
        in_specs=(P("blk", None, None, None), P("blk", "team", None), P("blk", None), P("blk")),
        out_specs=(P("blk", None, None, None), P("blk", "team", None)),
        check_vma=False,
    )
```

```python
import jax
import jax.numpy as jnp
from jax import lax
from jax.experimental import pallas as pl
from jax.experimental.pallas import tpu as pltpu
from jax.sharding import PartitionSpec as P

step_size = 0.1
penalty = 0.05
MESH = pl.DeviceIdType.MESH


def link_distances(row_total):
    reach_near = max(1, row_total // 16)
    far_count = max(1, row_total // 32)
    far_stride = max(1, (row_total // 2 - 1 - reach_near) // far_count)
    distances = [(0, False)]
    for distance in range(1, reach_near + 1):
        distances.append((distance, False))
        distances.append((-distance, False))
    for number in range(far_count):
        distance = row_total // 2 - number * far_stride
        distances.append((distance, True))
        if 2 * distance != row_total:
            distances.append((-distance, True))
    return distances


def split(value):
    high = value.astype(jnp.bfloat16)
    low = (value - high.astype(jnp.float32)).astype(jnp.bfloat16)
    return high, low


def make_kernel(row_total, team_size, slot_count, samples_here, size):
    distances = link_distances(row_total)
    tiles = len(distances)
    steps = [distance for distance, _ in distances]
    opposite = [t if 2 * abs(step) == row_total else steps.index(-step)
                for t, step in enumerate(steps)]
    used = min(slot_count, tiles)
    groups = team_size // 2
    half_rows = size // 2
    samples = samples_here * team_size

    def kernel(links_hbm, w_hbm, x_hbm, out_buf, y_out,
               links, w_buf, x_buf, part, pair_in, half, far_in, back_in, full, back,
               local_sem, x_send, x_recv, pair_send, pair_recv,
               far_send, far_recv, full_send, full_recv,
               row_send, row_recv, back_send, back_recv):
        row = lax.axis_index("blk")
        team = lax.axis_index("team")
        core = lax.rem(team, 2)
        group = team // 2
        other = group * 2 + (1 - core)
        mine = pl.ds(pl.multiple_of(core * half_rows, half_rows), half_rows)
        theirs = pl.ds(pl.multiple_of((1 - core) * half_rows, half_rows), half_rows)

        load_w = pltpu.make_async_copy(w_hbm.at[0, pl.ds(0, used)], w_buf, local_sem.at[0])
        load_w.start()
        load_x = pltpu.make_async_copy(x_hbm.at[0], x_buf.at[0], local_sem.at[1])
        load_x.start()
        load_links = pltpu.make_async_copy(links_hbm, links, local_sem.at[2])
        load_links.start()

        def target(t):
            distance, wraps = distances[t]
            there = row - distance
            ok = None if wraps else (there >= 0) & (there < row_total)
            return lax.rem(there + row_total, row_total), ok

        def source_ok(t):
            distance, wraps = distances[t]
            there = row + distance
            return None if wraps else (there >= 0) & (there < row_total)

        def guarded(ok, action):
            if ok is None:
                action()
            else:
                pl.when(ok)(action)

        def far_team(step):
            return lax.rem(group + step, groups) * 2 + core

        barrier = pltpu.get_barrier_semaphore()
        expected = jnp.int32(groups)
        for t in range(1, tiles):
            there, ok = target(t)

            def greet(there=there):
                for step in range(groups):
                    pl.semaphore_signal(barrier, inc=1, device_id=(there, far_team(step)),
                                        device_id_type=MESH)
            guarded(ok, greet)
            ok = source_ok(t)
            expected = expected + (groups if ok is None else groups * ok.astype(jnp.int32))
        pl.semaphore_signal(barrier, inc=1, device_id=(row, other), device_id_type=MESH)
        for step in range(1, groups):
            pl.semaphore_signal(barrier, inc=1, device_id=(row, far_team(step)), device_id_type=MESH)
        pl.semaphore_wait(barrier, expected)

        def exchange(source, buf, send, recv):
            copies = {}
            for t in reversed(range(1, tiles)):
                there, ok = target(t)
                copy = pltpu.make_async_remote_copy(
                    src_ref=source, dst_ref=buf.at[t], send_sem=send.at[t], recv_sem=recv.at[t],
                    device_id=(there, team), device_id_type=MESH)
                guarded(ok, copy.start)
                copies[t] = copy
            return copies

        def arrived(copies, buf, t):
            ok = source_ok(t)
            if ok is None:
                copies[t].wait_recv()
            else:
                pl.when(ok)(copies[t].wait_recv)

                def clear():
                    buf[t] = jnp.zeros_like(buf[t])
                pl.when(jnp.logical_not(ok))(clear)

        def sent(copies):
            for t in range(1, tiles):
                guarded(target(t)[1], copies[t].wait_send)

        load_x.wait()
        x_copies = exchange(x_buf.at[0], x_buf, x_send, x_recv)

        rest = slot_count - used
        if rest:
            out_buf[0, pl.ds(used, rest)] = jnp.zeros((rest, size, size), jnp.float32)

        load_links.wait()
        live_slot = [jnp.bool_(True)] + [links[0, k] > links[0, k - 1] for k in range(1, used)]
        slot_of, is_live = [], []
        for t in range(tiles):
            column = lax.rem(row + distances[t][0] + row_total, row_total)
            slot = jnp.int32(0)
            found = jnp.bool_(False)
            for k in range(used):
                hit = (links[0, k] == column) & live_slot[k]
                slot = jnp.where(hit, k, slot)
                found = found | hit
            slot_of.append(slot)
            is_live.append(found)

        load_w.wait()
        y = None
        for t in range(tiles):
            weight = jnp.where(is_live[t], w_buf[slot_of[t]], 0.0)
            w_high, w_low = split(weight)
            right = jnp.concatenate([w_high, w_low, w_high], axis=1)
            if t:
                arrived(x_copies, x_buf, t)
            high, low = split(x_buf[t])
            left = jnp.concatenate([high, high, low], axis=1)
            term = lax.dot_general(left, right, (((1,), (1,)), ((), ())),
                                   preferred_element_type=jnp.float32)
            y = term if y is None else y + term
        y_out[0] = y

        high, low = split(y)
        left = jnp.concatenate([high, high, low, low], axis=0).astype(jnp.float32).T
        left = left.astype(jnp.bfloat16)

        pair_copies, far_copies, full_copies, row_copies, back_copies = {}, {}, {}, {}, {}

        def stage_tile(t):
            high, low = split(x_buf[t])
            right = jnp.concatenate([high, low, high, low], axis=0)
            part[t] = jnp.dot(left, right, preferred_element_type=jnp.float32)
            pair_copies[t] = pltpu.make_async_remote_copy(
                src_ref=part.at[t, theirs], dst_ref=pair_in.at[t],
                send_sem=pair_send.at[t], recv_sem=pair_recv.at[t],
                device_id=(row, other), device_id_type=MESH)
            pair_copies[t].start()

        def stage_pair(t):
            pair_copies[t].wait_recv()
            half[t] = part[t, mine] + pair_in[t]
            if t:
                u = opposite[t]
                there, ok = target(u)
                row_copies[u] = [pltpu.make_async_remote_copy(
                    src_ref=half.at[t], dst_ref=back_in.at[step, u],
                    send_sem=row_send.at[step, u], recv_sem=row_recv.at[step, u],
                    device_id=(there, far_team(step)), device_id_type=MESH)
                    for step in range(groups)]

                def send_rows():
                    for copy in reversed(row_copies[u]):
                        copy.start()
                guarded(ok, send_rows)
            far_copies[t] = []
            for step in range(1, groups):
                copy = pltpu.make_async_remote_copy(
                    src_ref=half.at[t], dst_ref=far_in.at[step - 1, t],
                    send_sem=far_send.at[step - 1, t], recv_sem=far_recv.at[step - 1, t],
                    device_id=(row, far_team(step)), device_id_type=MESH)
                copy.start()
                far_copies[t].append(copy)

        def stage_far(t):
            total = half[t]
            for step in range(1, groups):
                far_copies[t][step - 1].wait_recv()
                total = total + far_in[step - 1, t]
            full[t, mine] = total
            full_copies[t] = pltpu.make_async_remote_copy(
                src_ref=full.at[t, mine], dst_ref=full.at[t, mine],
                send_sem=full_send.at[t], recv_sem=full_recv.at[t],
                device_id=(row, other), device_id_type=MESH)
            full_copies[t].start()

        def stage_back(u):
            back_copies[u] = pltpu.make_async_remote_copy(
                src_ref=back.at[u, mine], dst_ref=back.at[u, mine],
                send_sem=back_send.at[u], recv_sem=back_recv.at[u],
                device_id=(row, other), device_id_type=MESH)

            def forward():
                for copy in row_copies[u]:
                    copy.wait_recv()
                total = back_in[0, u]
                for step in range(1, groups):
                    total = total + back_in[step, u]
                back[u, mine] = total
                back_copies[u].start()
            guarded(source_ok(u), forward)

        order = list(reversed(range(tiles)))
        for i, t in enumerate(order):
            stage_tile(t)
            if i:
                stage_pair(order[i - 1])
        stage_pair(order[-1])
        for t in order:
            stage_far(t)
        for t in order[:-1]:
            stage_back(opposite[t])
        for t in order:
            full_copies[t].wait_recv()
        back[0] = full[0]
        for t in order[:-1]:
            guarded(source_ok(t), back_copies[t].wait_recv)

        diagonal = (lax.broadcasted_iota(jnp.int32, (size, size), 0)
                    == lax.broadcasted_iota(jnp.int32, (size, size), 1))
        for k in range(used):
            live = live_slot[k]
            column = links[0, k]
            place = jnp.int32(0)
            for t in range(1, tiles):
                hit = column == lax.rem(row + distances[t][0] + row_total, row_total)
                place = jnp.where(hit, t, place)
            weight = w_buf[k]
            grad = (full[place] + back[place].T) / (2.0 * samples)
            corner = diagonal & (live & (column == row))
            grad = grad - jnp.where(corner, 1.0 / jnp.where(corner, weight, 1.0), 0.0)
            moved = weight - step_size * grad
            edge = step_size * penalty
            shrunk = moved - jnp.minimum(jnp.maximum(moved, -edge), edge)
            result = jnp.where(corner, moved, shrunk)
            out_buf[0, k] = jnp.where(live, result, 0.0)

        sent(x_copies)
        for t in range(1, tiles):
            for copy in row_copies[t]:
                guarded(target(t)[1], copy.wait_send)
        for t in range(1, tiles):
            guarded(source_ok(t), back_copies[t].wait_send)
        for t in range(tiles):
            pair_copies[t].wait_send()
            for copy in far_copies[t]:
                copy.wait_send()
            full_copies[t].wait_send()

    f32 = jnp.float32
    far = max(1, groups - 1)
    dma = pltpu.SemaphoreType.DMA
    scratch = [
        pltpu.SMEM((1, slot_count), jnp.int32),
        pltpu.VMEM((used, size, size), f32),
        pltpu.VMEM((tiles, samples_here, size), f32),
        pltpu.VMEM((tiles, size, size), f32),
        pltpu.VMEM((tiles, half_rows, size), f32),
        pltpu.VMEM((tiles, half_rows, size), f32),
        pltpu.VMEM((far, tiles, half_rows, size), f32),
        pltpu.VMEM((groups, tiles, half_rows, size), f32),
        pltpu.VMEM((tiles, size, size), f32),
        pltpu.VMEM((tiles, size, size), f32),
        dma((3,)), dma((tiles,)), dma((tiles,)),
        dma((tiles,)), dma((tiles,)), dma((far, tiles)), dma((far, tiles)),
        dma((tiles,)), dma((tiles,)), dma((groups, tiles)), dma((groups, tiles)),
        dma((tiles,)), dma((tiles,)),
    ]
    return kernel, scratch


def write_out(omega_in, y_in, omega_out, y_out, sem):
    first = pltpu.make_async_copy(omega_in, omega_out, sem.at[0])
    second = pltpu.make_async_copy(y_in, y_out, sem.at[1])
    first.start()
    second.start()
    first.wait()
    second.wait()


def per_device(omega, dosage, columns, counts):
    row_total = lax.axis_size("blk")
    team_size = lax.axis_size("team")
    slot_count, size = omega.shape[1], omega.shape[2]
    samples_here = dosage.shape[1]
    kernel, scratch = make_kernel(row_total, team_size, slot_count, samples_here, size)
    shapes = (jax.ShapeDtypeStruct(omega.shape, jnp.float32),
              jax.ShapeDtypeStruct(dosage.shape, jnp.float32))
    results = pl.pallas_call(
        kernel,
        out_shape=shapes,
        in_specs=[pl.BlockSpec(memory_space=pltpu.HBM)] * 3,
        out_specs=(pl.BlockSpec(memory_space=pltpu.VMEM), pl.BlockSpec(memory_space=pltpu.VMEM)),
        scratch_shapes=scratch,
        compiler_params=pltpu.CompilerParams(
            collective_id=0, has_side_effects=True, vmem_limit_bytes=24 * 1024 * 1024),
    )(*[pltpu.with_memory_space_constraint(value, pltpu.HBM)
        for value in (columns, omega, dosage)])
    return pl.pallas_call(
        write_out,
        out_shape=shapes,
        in_specs=[pl.BlockSpec(memory_space=pl.ANY)] * 2,
        out_specs=(pl.BlockSpec(memory_space=pltpu.HBM), pl.BlockSpec(memory_space=pltpu.HBM)),
        scratch_shapes=[pltpu.SemaphoreType.DMA((2,))],
    )(*[pltpu.with_memory_space_constraint(value, pltpu.VMEM) for value in results])


def solution(mesh):
    return jax.shard_map(
        per_device,
        mesh=mesh,
        in_specs=(P("blk", None, None, None), P("blk", "team", None), P("blk", None), P("blk")),
        out_specs=(P("blk", None, None, None), P("blk", "team", None)),
        check_vma=False,
    )
```
